256 devices in a mesh: lm: 16 (over x_lo, z), node: 16 (over x_hi, y, core).
Axes of the slice: x: 4 (x_hi: 2, x_lo: 2; x = x_hi * 2 + x_lo), y: 4, z: 8, core: 2. Of those that a mesh axis runs over, the one named last changes fastest.
Arguments:
- features: bfloat16 [128, 262144], P(None, ('node', 'lm')), may hold values from -6 to 6
- landmarks: bfloat16 [128, 8192], P(None, ('lm', 'node')), may hold values from -6 to 6
- cotangent: bfloat16 [64, 262144], P(None, ('node', 'lm')), may hold values from -24 to 24
- eigen_basis: bfloat16 [64, 8192], P(None, ('lm', 'node')), may hold values from -0.5 to 0.5
- inv_eigen: float32 [64], replicated, may hold values from 0.5 to 8
Outputs:
- grad_features: float32 [128, 262144], P(None, ('node', 'lm'))
- grad_landmarks: float32 [128, 8192], P(None, ('lm', 'node'))
The draws below stay inside these ranges and needn't reach their ends.
All inputs are finite; a program needn't handle non-finite values.
Results may differ from the reference program's by a relative error of at most 0.004.
Values may be sent and summed in bfloat16 or wider, within the bound.
A program may use at most 64 MiB of HBM per device.

```python
import math
import jax
import jax.numpy as jnp
from jax import lax

F = 128
R = 64
M = 8192
N = 262144


def shard_levels(own_key, dims, pieces, least, top_value):
    def one(dim, blocks):
        steps = jax.random.uniform(jax.random.fold_in(jax.random.fold_in(own_key, 6), dim), (blocks,), jnp.float32, least / len(pieces), top_value / len(pieces))
        return jnp.repeat(jnp.exp(steps), dims[dim] // blocks).reshape((-1,) + (1,) * (len(dims) - dim - 1))

    loudness = one(*pieces[0])
    for cut in pieces[1:]:
        loudness = loudness * one(*cut)
    return loudness


def gaussian(stream_key, shape, spread, reach, pieces=(), kind=jnp.bfloat16):
    result = spread * jax.random.normal(stream_key, shape, jnp.float32)
    if pieces:
        result = result * shard_levels(stream_key, shape, pieces, -0.22, 0.18)
    return jnp.clip(result, -reach, reach).astype(kind)


def setup_inputs(seed: int = 0) -> dict:
    key_list = jax.random.split(jax.random.key(seed), 6)
    return {
        "features": gaussian(key_list[0], (F, N), 1.0, 6.0, ((1, 256),)),
        "landmarks": gaussian(key_list[1], (F, M), 1.0, 6.0, ((1, 256),)),
        "cotangent": gaussian(key_list[2], (R, N), 4.0, 24.0, ((1, 256),)),
        "eigen_basis": gaussian(key_list[3], (R, M), (M // 64) ** -0.5, 0.5, ((1, 256),)),
        "inv_eigen": jnp.clip(jnp.exp(jax.random.uniform(key_list[4], (R,), jnp.float32, math.log(0.5), math.log(8.0))), 0.5, 8.0),
    }


def tile_terms(node_rows, node_grads, marks, marks_square, projection, factor):
    rows_float = node_rows.astype(jnp.float32)
    cross = jnp.dot(node_rows.T, marks, preferred_element_type=jnp.float32)
    rows_square = jnp.sum(rows_float * rows_float, axis=0)
    kernel = jnp.exp(-(rows_square[:, None] + marks_square[None, :] - 2.0 * cross) * (0.5 * factor))
    pull = jnp.dot(node_grads.T, projection, preferred_element_type=jnp.float32)
    weight = pull * kernel
    weight_half = weight.astype(jnp.bfloat16)
    toward = factor * (jnp.dot(marks, weight_half.T, preferred_element_type=jnp.float32) - rows_float * jnp.sum(weight, axis=1)[None, :])
    backward_term = jnp.dot(node_rows, weight_half, preferred_element_type=jnp.float32)
    column_sums = jnp.sum(weight, axis=0)
    return toward, backward_term, column_sums


def reference(features, landmarks, cotangent, eigen_basis, inv_eigen):
    factor = 4.0 / F
    marks_float = landmarks.astype(jnp.float32)
    marks_square = jnp.sum(marks_float * marks_float, axis=0)
    projection = (inv_eigen[:, None] * eigen_basis.astype(jnp.float32)).astype(jnp.bfloat16)
    row_block = min(2048, N)

    def sweep(carry, index):
        start = (index * row_block).astype(jnp.int32)
        node_rows = lax.dynamic_slice_in_dim(features, start, row_block, 1)
        node_grads = lax.dynamic_slice_in_dim(cotangent, start, row_block, 1)
        toward, backward_term, column_sums = tile_terms(node_rows, node_grads, landmarks, marks_square, projection, factor)
        return (carry[0] + backward_term, carry[1] + column_sums), toward

    initial = (jnp.zeros((F, M), jnp.float32), jnp.zeros((M,), jnp.float32))
    totals, towards = lax.scan(sweep, initial, jnp.arange(N // row_block, dtype=jnp.int32))
    grad_features = jnp.transpose(towards, (1, 0, 2)).reshape(F, N)
    grad_landmarks = factor * (totals[0] - marks_float * totals[1][None, :])
    return grad_features, grad_landmarks
```

```python
import functools
import math

import jax
import jax.numpy as jnp
from jax import lax
from jax.experimental import pallas as pl
from jax.experimental.pallas import tpu as pltpu
from jax.sharding import PartitionSpec as P

MESH = pl.DeviceIdType.MESH
F32 = jnp.float32
BF16 = jnp.bfloat16
LAST = (((1,), (1,)), ((), ()))
ORDER = (1, 3, 2)
PASS = 512


def coordinates():
    lm, node = lax.axis_index("lm"), lax.axis_index("node")
    x, y, z, core = (lm // 8) + 2 * (node // 8), (node // 2) % 4, lm % 8, node % 2
    first = x * (1 - core) + y * core
    second = y * (1 - core) + x * core
    return first, second, z, core


def device(first, second, z, core, other=0):
    x = first * (1 - core) + second * core
    y = second * (1 - core) + first * core
    side = core * (1 - other) + (1 - core) * other
    return {"lm": (x % 2) * 8 + z, "node": (x // 2 * 4 + y) * 2 + side}


def pieces(rows, ones_first):
    square = jnp.sum(rows * rows, axis=1, keepdims=True) * -0.5
    high = square.astype(BF16).astype(F32)
    rest = square - high
    middle = rest.astype(BF16).astype(F32)
    low = rest - middle
    lane = lax.broadcasted_iota(jnp.int32, rows.shape, 1)
    at = 3 if ones_first else 0
    one = 0 if ones_first else 3
    zero = jnp.zeros(rows.shape, F32)
    out = jnp.where((lane >= one) & (lane < one + 3), 1.0, zero)
    out = jnp.where(lane == at, high, out)
    out = jnp.where(lane == at + 1, middle, out)
    out = jnp.where(lane == at + 2, low, out)
    return out.astype(BF16)


def kernel(
    factor, x_ref, l_ref, g_ref, e_ref, inv_ref, gf_ref, gl_ref,
    marks, mate_x, mate_g, rows, grads, wide, weights,
    send1, recv1, own, send2, recv2, send3, recv3, back, mate_back, mine,
    z_s, z_r, c_s, c_r, g_s, g_r, r1_s, r1_r, r2_s, r2_r, r3_s, r3_r, t_s, t_r,
):
    first, second, z, core = coordinates()
    half = x_ref.shape[1]

    def on_first(step):
        return device((first + step) % 4, second, z, core)

    def on_second(step):
        return device(first, (second + step) % 4, z, core)

    def on_z(step):
        return device(first, second, (z + step) % 8, core)

    mate = device(first, second, z, core, 1)

    def remote(src, dst, s, r, to):
        return pltpu.make_async_remote_copy(
            src_ref=src, dst_ref=dst, send_sem=s, recv_sem=r, device_id=to, device_id_type=MESH
        )

    barrier = pltpu.get_barrier_semaphore()
    partners = [on_z(d) for d in range(1, 8)]
    partners += [on_first(d) for d in range(1, 4)] + [on_second(d) for d in range(1, 4)] + [mate]
    for partner in partners:
        pl.semaphore_signal(barrier, inc=1, device_id=partner, device_id_type=MESH)

    at = pl.ds(pl.multiple_of(z * 16, 16), 16)
    own_rows = l_ref[...].astype(F32).T
    marks[0, 0, at, :] = own_rows[:16].astype(BF16)
    marks[0, 1, at, :] = own_rows[16:].astype(BF16)
    projection = e_ref[...].astype(F32).T * inv_ref[...]
    marks[0, 2, at, :] = jnp.concatenate([projection[:16], projection[16:]], axis=1).astype(BF16)

    pl.semaphore_wait(barrier, len(partners))
    sent = []

    def go(copy):
        copy.start()
        sent.append(copy)
        return copy

    z_in = [go(remote(marks.at[0, :, at, :], marks.at[0, :, at, :], z_s.at[d], z_r.at[d], on_z(d + 1))) for d in range(7)]
    x_in = go(remote(x_ref, mate_x, c_s.at[0], c_r.at[0], mate))
    g_in = go(remote(g_ref, mate_g, c_s.at[1], c_r.at[1], mate))

    def prepare(x, g, base):
        turned = x[...].astype(F32).T
        rows[base : base + half, :128] = turned.astype(BF16)
        rows[base : base + half, 128:] = pieces(turned, False)
        pulled = g[...].astype(F32).T
        grads[base : base + half, :] = jnp.concatenate([pulled, pulled], axis=1).astype(BF16)
        wide[:128, base : base + half] = x[...]

    prepare(x_ref, g_ref, 0)
    wide[128:, :] = (lax.broadcasted_iota(jnp.int32, (16, 2 * half), 0) == 0).astype(F32).astype(BF16)
    x_in.wait_recv()
    g_in.wait_recv()
    prepare(mate_x, mate_g, half)

    scale = factor * math.log2(math.e)

    def mark_rows(k):
        return marks[k, 0:2].reshape(256, 128)

    def weigh(k):
        plain = mark_rows(k)
        near = jnp.concatenate([plain, pieces(plain.astype(F32), True)], axis=1)
        packed = marks[k, 2]
        lane = lax.broadcasted_iota(jnp.int32, packed.shape, 1)
        zero = jnp.zeros_like(packed)
        pull = jnp.concatenate([jnp.where(lane < 64, packed, zero), jnp.where(lane < 64, zero, packed)], axis=0)
        cross = lax.dot_general(rows[...], near, LAST, preferred_element_type=F32)
        pulled = lax.dot_general(grads[...], pull, LAST, preferred_element_type=F32)
        weights[k] = (pulled * jnp.exp2(cross * scale)).astype(BF16)

    def backward(k):
        total = jnp.dot(wide[...], weights[k], preferred_element_type=F32).T
        return total[:, :128] - mark_rows(k).astype(F32) * total[:, 128:129]

    for c in z_in:
        c.wait_recv()
    incoming = {}
    for d in range(1, 4):
        incoming[d] = go(remote(marks.at[0], marks.at[d], g_s.at[d], g_r.at[d], on_first(-d + 4)))
    for d in ORDER:
        incoming[4 * d] = go(remote(marks.at[0], marks.at[4 * d], g_s.at[4 * d], g_r.at[4 * d], on_second(-d + 4)))
    weigh(0)
    for k in ORDER:
        incoming[k].wait_recv()
        for d in ORDER:
            s = 4 * d + k
            incoming[s] = go(remote(marks.at[k], marks.at[s], g_s.at[s], g_r.at[s], on_second(-d + 4)))
    for k in ORDER:
        weigh(k)

    reduce1 = []
    ready = []
    behind = None

    def ship():
        for k in ready:
            d, f = k // 4, k % 4
            n = (d - 1) * 4 + f
            reduce1.append(go(remote(send1.at[n], recv1.at[n], r1_s.at[n], r1_r.at[n], on_second(d))))
        ready.clear()

    def finish(k):
        send1[(k // 4 - 1) * 4 + k % 4] = backward(k).astype(BF16)
        ready.append(k)

    for d in ORDER:
        ship()
        for f in range(4):
            incoming[4 * d + f].wait_recv()
        for f in range(4):
            weigh(4 * d + f)
            if behind is not None:
                finish(behind)
            behind = 4 * d + f
    finish(behind)
    ship()
    for f in range(4):
        own[f] = backward(f)

    ones = (lax.broadcasted_iota(jnp.int32, (256, 128), 1) == 0).astype(F32).astype(BF16)

    def toward(r):
        total = jnp.zeros((PASS, 256), F32)
        for k in range(16):
            total = total + jnp.dot(
                weights[k, r : r + PASS, :], jnp.concatenate([mark_rows(k), ones], axis=1), preferred_element_type=F32
            )
        return total[:, :128] - rows[r : r + PASS, :128].astype(F32) * total[:, 128:129]

    for r in range(0, half, PASS):
        if r == PASS:
            for c in reduce1:
                c.wait_recv()
            reduce2 = []
            for f in (1, 3, 2, 0):
                total = own[f]
                for d in range(3):
                    total = total + recv1[d * 4 + f].astype(F32)
                if f:
                    send2[f - 1] = total
                    reduce2.append(go(remote(send2.at[f - 1], recv2.at[f - 1], r2_s.at[f - 1], r2_r.at[f - 1], on_first(f))))
                else:
                    own[0] = total
        back[r : r + PASS, :] = toward(half + r)
    t_in = go(remote(back, mate_back, t_s, t_r, mate))
    for r in range(0, half, PASS):
        if r == PASS:
            for c in reduce2:
                c.wait_recv()
            total = own[0] + recv2[0] + recv2[1] + recv2[2]
            send3[...] = total.reshape(2, 128, 128)
            reduce3 = []
            for d in range(7):
                to = (z + d + 1) % 8
                part = pl.ds(pl.multiple_of(to * 16, 16), 16)
                reduce3.append(go(remote(send3.at[:, part, :], recv3.at[d], r3_s.at[d], r3_r.at[d], on_z(d + 1))))
        mine[r : r + PASS, :] = toward(r)

    t_in.wait_recv()
    gf_ref[...] = factor * (mine[...] + mate_back[...]).T

    for c in reduce3:
        c.wait_recv()
    total = send3[:, at, :]
    for d in range(7):
        total = total + recv3[d]
    gl_ref[...] = factor * total.reshape(32, 128).T
    for c in sent:
        c.wait_send()


def per_device(features, landmarks, cotangent, eigen_basis, inv_eigen):
    width, count = features.shape
    vmem = pl.BlockSpec(memory_space=pltpu.VMEM)
    dma = pltpu.SemaphoreType.DMA
    return pl.pallas_call(
        functools.partial(kernel, 4.0 / width),
        out_shape=(
            jax.ShapeDtypeStruct(features.shape, F32),
            jax.ShapeDtypeStruct(landmarks.shape, F32),
        ),
        in_specs=[vmem] * 5,
        out_specs=(vmem, vmem),
        scratch_shapes=[
            pltpu.VMEM((16, 3, 128, 128), BF16),
            pltpu.VMEM((128, count), BF16),
            pltpu.VMEM((64, count), BF16),
            pltpu.VMEM((2 * count, 256), BF16),
            pltpu.VMEM((2 * count, 128), BF16),
            pltpu.VMEM((144, 2 * count), BF16),
            pltpu.VMEM((16, 2 * count, 256), BF16),
            pltpu.VMEM((12, 256, 128), BF16),
            pltpu.VMEM((12, 256, 128), BF16),
            pltpu.VMEM((4, 256, 128), F32),
            pltpu.VMEM((3, 256, 128), F32),
            pltpu.VMEM((3, 256, 128), F32),
            pltpu.VMEM((2, 128, 128), F32),
            pltpu.VMEM((7, 2, 16, 128), F32),
            pltpu.VMEM((count, 128), F32),
            pltpu.VMEM((count, 128), F32),
            pltpu.VMEM((count, 128), F32),
            dma((7,)), dma((7,)), dma((2,)), dma((2,)), dma((16,)), dma((16,)),
            dma((12,)), dma((12,)), dma((3,)), dma((3,)), dma((7,)), dma((7,)), dma, dma,
        ],
        compiler_params=pltpu.CompilerParams(
            collective_id=0, has_side_effects=True, vmem_limit_bytes=60 * 2**20
        ),
    )(features, landmarks, cotangent, eigen_basis, inv_eigen.reshape(1, -1))


def solution(mesh):
    return jax.shard_map(
        per_device,
        mesh=mesh,
        in_specs=(
            P(None, ("node", "lm")),
            P(None, ("lm", "node")),
            P(None, ("node", "lm")),
            P(None, ("lm", "node")),
            P(),
        ),
        out_specs=(P(None, ("node", "lm")), P(None, ("lm", "node"))),
        check_vma=False,
    )
```

```python
import functools
import math

import jax
import jax.numpy as jnp
from jax import lax
from jax.experimental import pallas as pl
from jax.experimental.pallas import tpu as pltpu
from jax.sharding import PartitionSpec as P

MESH = pl.DeviceIdType.MESH
F32 = jnp.float32
BF16 = jnp.bfloat16
LAST = (((1,), (1,)), ((), ()))
PLANE = (
    (0, 0), (1, 0), (0, 1), (3, 0), (0, 3), (1, 1), (3, 3), (3, 1), (1, 3),
    (2, 0), (0, 2), (2, 1), (1, 2), (2, 3), (3, 2), (2, 2),
)
EARLY = 4
PASS = 512


def coordinates():
    lm, node = lax.axis_index("lm"), lax.axis_index("node")
    return (lm // 8) + 2 * (node // 8), (node // 2) % 4, lm % 8, node % 2


def device(x, y, z, core):
    return {"lm": (x % 2) * 8 + z, "node": (x // 2 * 4 + y) * 2 + core}


def pieces(rows, ones_first):
    square = jnp.sum(rows * rows, axis=1, keepdims=True) * -0.5
    high = square.astype(BF16).astype(F32)
    rest = square - high
    middle = rest.astype(BF16).astype(F32)
    low = rest - middle
    lane = lax.broadcasted_iota(jnp.int32, rows.shape, 1)
    at = 3 if ones_first else 0
    one = 0 if ones_first else 3
    zero = jnp.zeros(rows.shape, F32)
    out = jnp.where((lane >= one) & (lane < one + 3), 1.0, zero)
    out = jnp.where(lane == at, high, out)
    out = jnp.where(lane == at + 1, middle, out)
    out = jnp.where(lane == at + 2, low, out)
    return out.astype(BF16)


def kernel(
    factor, x_ref, l_ref, g_ref, e_ref, inv_ref, gf_ref, gl_ref,
    marks, mate_x, mate_g, far_x, far_g, cross_x, cross_g, rows, grads, wide, weights,
    send1, recv1, own, send3, recv3, part, mate_part, send4, recv4, back, mate_back, mine,
    z_s, z_r, c_s, c_r, g_s, g_r, r1_s, r1_r, r3_s, r3_r, t_s, t_r,
):
    x, y, z, core = coordinates()
    half = x_ref.shape[1]
    level = z // 2
    chip = 2 * half

    def in_plane(i, sign):
        return device((x + 4 + sign * PLANE[i][0]) % 4, (y + 4 + sign * PLANE[i][1]) % 4, z, core)

    def on_z(step):
        return device(x, y, (z + 2 * step) % 8, core)

    mate = device(x, y, z, 1 - core)
    far = device(x, y, z + 1 - 2 * (z % 2), core)

    def remote(src, dst, s, r, to):
        return pltpu.make_async_remote_copy(
            src_ref=src, dst_ref=dst, send_sem=s, recv_sem=r, device_id=to, device_id_type=MESH
        )

    barrier = pltpu.get_barrier_semaphore()
    partners = [on_z(d) for d in range(1, 4)] + [in_plane(i, 1) for i in range(1, 16)] + [mate, far]
    for partner in partners:
        pl.semaphore_signal(barrier, inc=1, device_id=partner, device_id_type=MESH)

    at = pl.ds(pl.multiple_of(level * 16, 16), 16)
    marks[0, 0, at, :] = l_ref[:16, :]
    marks[0, 1, at, :] = l_ref[16:, :]
    projection = e_ref[...].astype(F32) * inv_ref[...]
    marks[0, 2, at, :] = jnp.concatenate([projection[:16], projection[16:]], axis=1).astype(BF16)

    pl.semaphore_wait(barrier, len(partners))
    sent = []

    def go(copy):
        copy.start()
        sent.append(copy)
        return copy

    z_in = [go(remote(marks.at[0, :, at, :], marks.at[0, :, at, :], z_s.at[d], z_r.at[d], on_z(d + 1))) for d in range(3)]
    x_in = go(remote(x_ref, mate_x, c_s.at[0], c_r.at[0], mate))
    g_in = go(remote(g_ref, mate_g, c_s.at[1], c_r.at[1], mate))
    far_in = [
        go(remote(x_ref, far_x, c_s.at[2], c_r.at[2], far)),
        go(remote(g_ref, far_g, c_s.at[3], c_r.at[3], far)),
    ]

    def prepare(x, g, base):
        turned = x[...].astype(F32).T
        rows[base : base + half, :128] = turned.astype(BF16)
        rows[base : base + half, 128:] = pieces(turned, False)
        pulled = g[...].astype(F32).T
        grads[base : base + half, :] = jnp.concatenate([pulled, pulled], axis=1).astype(BF16)
        wide[:128, base : base + half] = x[...]

    prepare(x_ref, g_ref, 0)
    wide[128:, :] = (lax.broadcasted_iota(jnp.int32, (16, 2 * chip), 0) == 0).astype(F32).astype(BF16)
    for c in z_in:
        c.wait_recv()
    incoming = {}
    for i in range(1, 16):
        incoming[i] = go(remote(marks.at[0], marks.at[i], g_s.at[i], g_r.at[i], in_plane(i, -1)))
    x_in.wait_recv()
    g_in.wait_recv()
    prepare(mate_x, mate_g, half)

    scale = factor * math.log2(math.e)

    def mark_rows(p):
        return marks[2 * p : 2 * p + 2, 0:2].reshape(256, 128)

    def weigh(p, base):
        plain = mark_rows(p)
        near = jnp.concatenate([plain, pieces(plain.astype(F32), True)], axis=1)
        pull = []
        for i in (2 * p, 2 * p + 1):
            packed = marks[i, 2]
            lane = lax.broadcasted_iota(jnp.int32, packed.shape, 1)
            zero = jnp.zeros_like(packed)
            pull += [jnp.where(lane < 64, packed, zero), jnp.where(lane < 64, zero, packed)]
        pull = jnp.concatenate(pull, axis=0)
        cross = lax.dot_general(rows[base : base + chip, :], near, LAST, preferred_element_type=F32)
        pulled = lax.dot_general(grads[base : base + chip, :], pull, LAST, preferred_element_type=F32)
        weights[p, base : base + chip, :] = (pulled * jnp.exp2(cross * scale)).astype(BF16)

    def backward(p):
        total = jnp.dot(wide[...], weights[p], preferred_element_type=F32).T
        return total[:, :128] - mark_rows(p).astype(F32) * total[:, 128:129]

    reduce1 = {}

    def finish(p):
        total = backward(p)
        for i in (2 * p, 2 * p + 1):
            block = total[(i % 2) * 128 : (i % 2) * 128 + 128]
            if i:
                send1[i] = block.astype(BF16)
            else:
                own[...] = block

    def ship(p):
        for i in (2 * p, 2 * p + 1):
            if i:
                reduce1[i] = go(remote(send1.at[i], recv1.at[i], r1_s.at[i], r1_r.at[i], in_plane(i, 1)))

    def arrived(p):
        for i in (2 * p, 2 * p + 1):
            if i:
                incoming[i].wait_recv()

    for p in range(EARLY):
        arrived(p)
        weigh(p, 0)
    for c in far_in:
        c.wait_recv()
    cross_in = [
        go(remote(far_x, cross_x, c_s.at[4], c_r.at[4], mate)),
        go(remote(far_g, cross_g, c_s.at[5], c_r.at[5], mate)),
    ]
    prepare(far_x, far_g, chip)
    arrived(EARLY)
    weigh(EARLY, 0)
    for c in cross_in:
        c.wait_recv()
    prepare(cross_x, cross_g, chip + half)
    for p in range(EARLY + 1):
        weigh(p, chip)
        if p:
            finish(p - 1)
    for p in range(EARLY):
        ship(p)
    for p in range(EARLY + 1, 8):
        arrived(p)
        weigh(p, 0)
        finish(p - 1)
        weigh(p, chip)
        ship(p - 1)
    finish(7)
    ship(7)

    ones = (lax.broadcasted_iota(jnp.int32, (256, 128), 1) == 0).astype(F32).astype(BF16)

    def toward(r):
        total = jnp.zeros((PASS, 256), F32)
        for p in range(8):
            total = total + jnp.dot(
                weights[p, r : r + PASS, :], jnp.concatenate([mark_rows(p), ones], axis=1), preferred_element_type=F32
            )
        return total[:, :128] - rows[r : r + PASS, :128].astype(F32) * total[:, 128:129]

    for r in range(0, half, PASS):
        part[r : r + PASS, :] = toward(chip + half + r)
    part_in = go(remote(part, mate_part, t_s.at[0], t_r.at[0], mate))
    for r in range(0, half, PASS):
        mine[r : r + PASS, :] = toward(chip + r)
    part_in.wait_recv()
    send4[...] = (mine[...] + mate_part[...]).astype(BF16)
    far_back = go(remote(send4, recv4, t_s.at[1], t_r.at[1], far))

    for i in range(1, 16):
        reduce1[i].wait_recv()
    total = own[...]
    for i in range(1, 16):
        total = total + recv1[i].astype(F32)
    send3[...] = total.reshape(2, 64, 128)
    reduce3 = []
    for d in range(3):
        to = pl.ds(pl.multiple_of((level + d + 1) % 4 * 16, 16), 16)
        reduce3.append(go(remote(send3.at[:, to, :], recv3.at[d], r3_s.at[d], r3_r.at[d], on_z(d + 1))))

    for r in range(0, half, PASS):
        back[r : r + PASS, :] = toward(half + r)
    t_in = go(remote(back, mate_back, t_s.at[2], t_r.at[2], mate))
    for r in range(0, half, PASS):
        mine[r : r + PASS, :] = toward(r)

    for c in reduce3:
        c.wait_recv()
    total = send3[:, at, :]
    for d in range(3):
        total = total + recv3[d]
    gl_ref[...] = factor * total.reshape(32, 128)
    t_in.wait_recv()
    far_back.wait_recv()
    gf_ref[...] = factor * (mine[...] + mate_back[...] + recv4[...].astype(F32)).T
    for c in sent:
        c.wait_send()


def per_device(features, landmarks, cotangent, eigen_basis, inv_eigen):
    width, count = features.shape
    vmem = pl.BlockSpec(memory_space=pltpu.VMEM)
    dma = pltpu.SemaphoreType.DMA
    grad_features, grad_landmarks = pl.pallas_call(
        functools.partial(kernel, 4.0 / width),
        out_shape=(
            jax.ShapeDtypeStruct(features.shape, F32),
            jax.ShapeDtypeStruct(landmarks.shape[::-1], F32),
        ),
        in_specs=[vmem] * 5,
        out_specs=(vmem, vmem),
        scratch_shapes=[
            pltpu.VMEM((16, 3, 64, 128), BF16),
            pltpu.VMEM((128, count), BF16),
            pltpu.VMEM((64, count), BF16),
            pltpu.VMEM((128, count), BF16),
            pltpu.VMEM((64, count), BF16),
            pltpu.VMEM((128, count), BF16),
            pltpu.VMEM((64, count), BF16),
            pltpu.VMEM((4 * count, 256), BF16),
            pltpu.VMEM((4 * count, 128), BF16),
            pltpu.VMEM((144, 4 * count), BF16),
            pltpu.VMEM((8, 4 * count, 256), BF16),
            pltpu.VMEM((16, 128, 128), BF16),
            pltpu.VMEM((16, 128, 128), BF16),
            pltpu.VMEM((128, 128), F32),
            pltpu.VMEM((2, 64, 128), F32),
            pltpu.VMEM((3, 2, 16, 128), F32),
            pltpu.VMEM((count, 128), F32),
            pltpu.VMEM((count, 128), F32),
            pltpu.VMEM((count, 128), BF16),
            pltpu.VMEM((count, 128), BF16),
            pltpu.VMEM((count, 128), F32),
            pltpu.VMEM((count, 128), F32),
            pltpu.VMEM((count, 128), F32),
            dma((3,)), dma((3,)), dma((6,)), dma((6,)), dma((16,)), dma((16,)),
            dma((16,)), dma((16,)), dma((3,)), dma((3,)), dma((3,)), dma((3,)),
        ],
        compiler_params=pltpu.CompilerParams(
            collective_id=0, has_side_effects=True, vmem_limit_bytes=60 * 2**20
        ),
    )(features, landmarks.T, cotangent, eigen_basis.T, inv_eigen.reshape(1, -1))
    return grad_features, grad_landmarks.T


def solution(mesh):
    return jax.shard_map(
        per_device,
        mesh=mesh,
        in_specs=(
            P(None, ("node", "lm")),
            P(None, ("lm", "node")),
            P(None, ("node", "lm")),
            P(None, ("lm", "node")),
            P(),
        ),
        out_specs=(P(None, ("node", "lm")), P(None, ("lm", "node"))),
        check_vma=False,
    )
```

```python
import functools
import math

import jax
import jax.numpy as jnp
from jax import lax
from jax.experimental import pallas as pl
from jax.experimental.pallas import tpu as pltpu
from jax.sharding import PartitionSpec as P

MESH = pl.DeviceIdType.MESH
F32 = jnp.float32
BF16 = jnp.bfloat16
LAST = (((1,), (1,)), ((), ()))
PLANE = (
    (0, 0), (1, 0), (0, 1), (3, 0), (0, 3), (1, 1), (3, 3), (3, 1), (1, 3),
    (2, 0), (0, 2), (2, 1), (1, 2), (2, 3), (3, 2), (2, 2),
)
PASS = 512


def coordinates():
    lm, node = lax.axis_index("lm"), lax.axis_index("node")
    return (lm // 8) + 2 * (node // 8), (node // 2) % 4, lm % 8, node % 2


def device(x, y, z, core):
    return {"lm": (x % 2) * 8 + z, "node": (x // 2 * 4 + y) * 2 + core}


def pieces(rows, ones_first):
    square = jnp.sum(rows * rows, axis=1, keepdims=True) * -0.5
    high = square.astype(BF16).astype(F32)
    rest = square - high
    middle = rest.astype(BF16).astype(F32)
    low = rest - middle
    lane = lax.broadcasted_iota(jnp.int32, rows.shape, 1)
    at = 3 if ones_first else 0
    one = 0 if ones_first else 3
    zero = jnp.zeros(rows.shape, F32)
    out = jnp.where((lane >= one) & (lane < one + 3), 1.0, zero)
    out = jnp.where(lane == at, high, out)
    out = jnp.where(lane == at + 1, middle, out)
    out = jnp.where(lane == at + 2, low, out)
    return out.astype(BF16)


def kernel(
    factor, x_ref, l_ref, g_ref, e_ref, inv_ref, gf_ref, gl_ref,
    marks, mate_x, mate_g, far_x, far_g, cross_x, cross_g, rows, grads, wide, weights,
    send1, recv1, own, send3, recv3, part, mate_part, send4, recv4, back, mate_back, mine,
    z_s, z_r, c_s, c_r, g_s, g_r, r1_s, r1_r, r3_s, r3_r, t_s, t_r,
):
    x, y, z, core = coordinates()
    half = x_ref.shape[1]
    level = z // 2
    chip = 2 * half

    def in_plane(i, sign):
        return device((x + 4 + sign * PLANE[i][0]) % 4, (y + 4 + sign * PLANE[i][1]) % 4, z, core)

    def on_z(step):
        return device(x, y, (z + 2 * step) % 8, core)

    mate = device(x, y, z, 1 - core)
    far = device(x, y, z + 1 - 2 * (z % 2), core)

    def remote(src, dst, s, r, to):
        return pltpu.make_async_remote_copy(
            src_ref=src, dst_ref=dst, send_sem=s, recv_sem=r, device_id=to, device_id_type=MESH
        )

    barrier = pltpu.get_barrier_semaphore()
    partners = [on_z(d) for d in range(1, 4)] + [in_plane(i, 1) for i in range(1, 16)] + [mate, far]
    for partner in partners:
        pl.semaphore_signal(barrier, inc=1, device_id=partner, device_id_type=MESH)

    at = pl.ds(pl.multiple_of(level * 16, 16), 16)
    marks[0, 0, at, :] = l_ref[:16, :]
    marks[0, 1, at, :] = l_ref[16:, :]
    projection = e_ref[...].astype(F32) * inv_ref[...]
    marks[0, 2, at, :] = jnp.concatenate([projection[:16], projection[16:]], axis=1).astype(BF16)

    pl.semaphore_wait(barrier, len(partners))
    sent = []

    def go(copy):
        copy.start()
        sent.append(copy)
        return copy

    z_in = [go(remote(marks.at[0, :, at, :], marks.at[0, :, at, :], z_s.at[d], z_r.at[d], on_z(d + 1))) for d in range(3)]
    x_in = go(remote(x_ref, mate_x, c_s.at[0], c_r.at[0], mate))
    g_in = go(remote(g_ref, mate_g, c_s.at[1], c_r.at[1], mate))
    far_in = [
        go(remote(x_ref, far_x, c_s.at[2], c_r.at[2], far)),
        go(remote(g_ref, far_g, c_s.at[3], c_r.at[3], far)),
    ]

    def prepare(x, g, base):
        turned = x[...].astype(F32).T
        rows[base : base + half, :128] = turned.astype(BF16)
        rows[base : base + half, 128:] = pieces(turned, False)
        pulled = g[...].astype(F32).T
        grads[base : base + half, :] = jnp.concatenate([pulled, pulled], axis=1).astype(BF16)
        wide[:128, base : base + half] = x[...]

    prepare(x_ref, g_ref, 0)
    wide[128:, :] = (lax.broadcasted_iota(jnp.int32, (16, 2 * chip), 0) == 0).astype(F32).astype(BF16)
    for c in z_in:
        c.wait_recv()
    incoming = {}

    def offer(*blocks):
        for i in blocks:
            incoming[i] = go(remote(marks.at[0], marks.at[i], g_s.at[i], g_r.at[i], in_plane(i, -1)))

    offer(1, 2, 3, 4)
    x_in.wait_recv()
    g_in.wait_recv()
    prepare(mate_x, mate_g, half)
    offer(5, 6, 7, 8)

    scale = factor * math.log2(math.e)

    def mark_rows(p):
        return marks[2 * p : 2 * p + 2, 0:2].reshape(256, 128)

    def weigh(p, base):
        plain = mark_rows(p)
        near = jnp.concatenate([plain, pieces(plain.astype(F32), True)], axis=1)
        pull = []
        for i in (2 * p, 2 * p + 1):
            packed = marks[i, 2]
            lane = lax.broadcasted_iota(jnp.int32, packed.shape, 1)
            zero = jnp.zeros_like(packed)
            pull += [jnp.where(lane < 64, packed, zero), jnp.where(lane < 64, zero, packed)]
        pull = jnp.concatenate(pull, axis=0)
        cross = lax.dot_general(rows[base : base + chip, :], near, LAST, preferred_element_type=F32)
        pulled = lax.dot_general(grads[base : base + chip, :], pull, LAST, preferred_element_type=F32)
        weights[p, base : base + chip, :] = (pulled * jnp.exp2(cross * scale)).astype(BF16)

    def backward(p):
        total = jnp.dot(wide[...], weights[p], preferred_element_type=F32).T
        return total[:, :128] - mark_rows(p).astype(F32) * total[:, 128:129]

    reduce1 = {}

    def finish(p):
        total = backward(p)
        for i in (2 * p, 2 * p + 1):
            block = total[(i % 2) * 128 : (i % 2) * 128 + 128]
            if i:
                send1[i] = block.astype(BF16)
            else:
                own[...] = block

    def ship(p):
        for i in (2 * p, 2 * p + 1):
            if i:
                reduce1[i] = go(remote(send1.at[i], recv1.at[i], r1_s.at[i], r1_r.at[i], in_plane(i, 1)))

    def arrived(p):
        for i in (2 * p, 2 * p + 1):
            if i:
                incoming[i].wait_recv()

    ones = (lax.broadcasted_iota(jnp.int32, (256, 128), 1) == 0).astype(F32).astype(BF16)

    def toward(r):
        total = jnp.zeros((PASS, 256), F32)
        for p in range(8):
            total = total + jnp.dot(
                weights[p, r : r + PASS, :], jnp.concatenate([mark_rows(p), ones], axis=1), preferred_element_type=F32
            )
        return total[:, :128] - rows[r : r + PASS, :128].astype(F32) * total[:, 128:129]

    arrived(0)
    arrived(1)
    offer(9, 10, 11)
    weigh(0, 0)
    weigh(1, 0)
    arrived(2)
    arrived(3)
    offer(12, 13, 14, 15)
    weigh(2, 0)
    weigh(3, 0)
    for c in far_in:
        c.wait_recv()
    cross_in = [
        go(remote(far_x, cross_x, c_s.at[4], c_r.at[4], mate)),
        go(remote(far_g, cross_g, c_s.at[5], c_r.at[5], mate)),
    ]
    arrived(4)
    prepare(far_x, far_g, chip)
    weigh(4, 0)
    for c in cross_in:
        c.wait_recv()
    prepare(cross_x, cross_g, chip + half)
    for p in range(4):
        weigh(p, chip)
        if p:
            finish(p - 1)
    for p in range(3):
        ship(p)
    arrived(5)
    weigh(4, chip)
    finish(3)
    weigh(5, 0)
    finish(4)
    weigh(5, chip)
    ship(3)
    ship(4)
    arrived(6)
    arrived(7)
    weigh(6, 0)
    finish(5)
    weigh(6, chip)
    weigh(7, 0)
    finish(6)
    weigh(7, chip)
    ship(5)
    ship(6)
    finish(7)
    ship(7)

    part_in = []
    for n in range(2):
        r = pl.ds(n * PASS, PASS)
        part[r, :] = toward(chip + half + n * PASS)
        part_in.append(go(remote(part.at[r, :], mate_part.at[r, :], t_s.at[n], t_r.at[n], mate)))
    far_back = []

    def send_back(n):
        r = pl.ds(n * PASS, PASS)
        part_in[n].wait_recv()
        send4[r, :] = (mine[r, :] + mate_part[r, :]).astype(BF16)
        far_back.append(go(remote(send4.at[r, :], recv4.at[r, :], t_s.at[2 + n], t_r.at[2 + n], far)))

    mine[:PASS, :] = toward(chip)
    send_back(0)
    mine[PASS:, :] = toward(chip + PASS)
    for r in range(0, half, PASS):
        back[r : r + PASS, :] = toward(half + r)
    t_in = go(remote(back, mate_back, t_s.at[4], t_r.at[4], mate))

    for i in range(1, 16):
        reduce1[i].wait_recv()
    total = own[...]
    for i in range(1, 16):
        total = total + recv1[i].astype(F32)
    send3[...] = total.reshape(2, 64, 128)
    reduce3 = []
    for d in range(3):
        to = pl.ds(pl.multiple_of((level + d + 1) % 4 * 16, 16), 16)
        reduce3.append(go(remote(send3.at[:, to, :], recv3.at[d], r3_s.at[d], r3_r.at[d], on_z(d + 1))))
    send_back(1)

    for r in range(0, half, PASS):
        mine[r : r + PASS, :] = toward(r)

    for c in reduce3:
        c.wait_recv()
    total = send3[:, at, :]
    for d in range(3):
        total = total + recv3[d]
    gl_ref[...] = factor * total.reshape(32, 128)
    t_in.wait_recv()
    for c in far_back:
        c.wait_recv()
    gf_ref[...] = factor * (mine[...] + mate_back[...] + recv4[...].astype(F32)).T
    for c in sent:
        c.wait_send()


def per_device(features, landmarks, cotangent, eigen_basis, inv_eigen):
    width, count = features.shape
    vmem = pl.BlockSpec(memory_space=pltpu.VMEM)
    dma = pltpu.SemaphoreType.DMA
    grad_features, grad_landmarks = pl.pallas_call(
        functools.partial(kernel, 4.0 / width),
        out_shape=(
            jax.ShapeDtypeStruct(features.shape, F32),
            jax.ShapeDtypeStruct(landmarks.shape[::-1], F32),
        ),
        in_specs=[vmem] * 5,
        out_specs=(vmem, vmem),
        scratch_shapes=[
            pltpu.VMEM((16, 3, 64, 128), BF16),
            pltpu.VMEM((128, count), BF16),
            pltpu.VMEM((64, count), BF16),
            pltpu.VMEM((128, count), BF16),
            pltpu.VMEM((64, count), BF16),
            pltpu.VMEM((128, count), BF16),
            pltpu.VMEM((64, count), BF16),
            pltpu.VMEM((4 * count, 256), BF16),
            pltpu.VMEM((4 * count, 128), BF16),
            pltpu.VMEM((144, 4 * count), BF16),
            pltpu.VMEM((8, 4 * count, 256), BF16),
            pltpu.VMEM((16, 128, 128), BF16),
            pltpu.VMEM((16, 128, 128), BF16),
            pltpu.VMEM((128, 128), F32),
            pltpu.VMEM((2, 64, 128), F32),
            pltpu.VMEM((3, 2, 16, 128), F32),
            pltpu.VMEM((count, 128), F32),
            pltpu.VMEM((count, 128), F32),
            pltpu.VMEM((count, 128), BF16),
            pltpu.VMEM((count, 128), BF16),
            pltpu.VMEM((count, 128), F32),
            pltpu.VMEM((count, 128), F32),
            pltpu.VMEM((count, 128), F32),
            dma((3,)), dma((3,)), dma((6,)), dma((6,)), dma((16,)), dma((16,)),
            dma((16,)), dma((16,)), dma((3,)), dma((3,)), dma((5,)), dma((5,)),
        ],
        compiler_params=pltpu.CompilerParams(
            collective_id=0, has_side_effects=True, vmem_limit_bytes=60 * 2**20
        ),
    )(features, landmarks.T, cotangent, eigen_basis.T, inv_eigen.reshape(1, -1))
    return grad_features, grad_landmarks.T


def solution(mesh):
    return jax.shard_map(
        per_device,
        mesh=mesh,
        in_specs=(
            P(None, ("node", "lm")),
            P(None, ("lm", "node")),
            P(None, ("node", "lm")),
            P(None, ("lm", "node")),
            P(),
        ),
        out_specs=(P(None, ("node", "lm")), P(None, ("lm", "node"))),
        check_vma=False,
    )
```

```python
import functools
import math

import jax
import jax.numpy as jnp
from jax import lax
from jax.experimental import pallas as pl
from jax.experimental.pallas import tpu as pltpu
from jax.sharding import PartitionSpec as P

MESH = pl.DeviceIdType.MESH
F32 = jnp.float32
BF16 = jnp.bfloat16
LAST = (((1,), (1,)), ((), ()))
PLANE = (
    (0, 0), (1, 0), (0, 1), (3, 0), (0, 3), (1, 1), (3, 3), (3, 1), (1, 3),
    (2, 0), (0, 2), (2, 1), (1, 2), (2, 3), (3, 2), (2, 2),
)
PASS = 512


def coordinates():
    lm, node = lax.axis_index("lm"), lax.axis_index("node")
    return (lm // 8) + 2 * (node // 8), (node // 2) % 4, lm % 8, node % 2


def device(x, y, z, core):
    return {"lm": (x % 2) * 8 + z, "node": (x // 2 * 4 + y) * 2 + core}


def pieces(rows, ones_first):
    square = jnp.sum(rows * rows, axis=1, keepdims=True) * -0.5
    high = square.astype(BF16).astype(F32)
    rest = square - high
    middle = rest.astype(BF16).astype(F32)
    low = rest - middle
    lane = lax.broadcasted_iota(jnp.int32, rows.shape, 1)
    at = 3 if ones_first else 0
    one = 0 if ones_first else 3
    zero = jnp.zeros(rows.shape, F32)
    out = jnp.where((lane >= one) & (lane < one + 3), 1.0, zero)
    out = jnp.where(lane == at, high, out)
    out = jnp.where(lane == at + 1, middle, out)
    out = jnp.where(lane == at + 2, low, out)
    return out.astype(BF16)


def kernel(
    factor, x_ref, l_ref, g_ref, e_ref, inv_ref, gf_ref, gl_ref,
    marks, mate_x, mate_g, far_x, far_g, cross_x, cross_g, rows, grads, wide, weights,
    send1, recv1, own, send3, recv3, part, mate_part, send4, recv4, back, mate_back, mine,
    z_s, z_r, c_s, c_r, g_s, g_r, r1_s, r1_r, r3_s, r3_r, t_s, t_r,
):
    x, y, z, core = coordinates()
    half = x_ref.shape[1]
    level = z // 2
    chip = 2 * half

    def in_plane(i, sign):
        return device((x + 4 + sign * PLANE[i][0]) % 4, (y + 4 + sign * PLANE[i][1]) % 4, z, core)

    def on_z(step):
        return device(x, y, (z + 2 * step) % 8, core)

    mate = device(x, y, z, 1 - core)
    far = device(x, y, z + 1 - 2 * (z % 2), core)

    def remote(src, dst, s, r, to):
        return pltpu.make_async_remote_copy(
            src_ref=src, dst_ref=dst, send_sem=s, recv_sem=r, device_id=to, device_id_type=MESH
        )

    barrier = pltpu.get_barrier_semaphore()
    partners = [on_z(d) for d in range(1, 4)] + [in_plane(i, 1) for i in range(1, 16)] + [mate, far]
    for partner in partners:
        pl.semaphore_signal(barrier, inc=1, device_id=partner, device_id_type=MESH)

    at = pl.ds(pl.multiple_of(level * 16, 16), 16)
    marks[0, 0, at, :] = l_ref[:16, :]
    marks[0, 1, at, :] = l_ref[16:, :]
    projection = e_ref[...].astype(F32) * inv_ref[...]
    marks[0, 2, at, :] = jnp.concatenate([projection[:16], projection[16:]], axis=1).astype(BF16)

    pl.semaphore_wait(barrier, len(partners))
    sent = []

    def go(copy):
        copy.start()
        sent.append(copy)
        return copy

    z_in = [go(remote(marks.at[0, :, at, :], marks.at[0, :, at, :], z_s.at[d], z_r.at[d], on_z(d + 1))) for d in range(3)]
    x_in = go(remote(x_ref, mate_x, c_s.at[0], c_r.at[0], mate))
    g_in = go(remote(g_ref, mate_g, c_s.at[1], c_r.at[1], mate))
    far_in = [
        go(remote(x_ref, far_x, c_s.at[2], c_r.at[2], far)),
        go(remote(g_ref, far_g, c_s.at[3], c_r.at[3], far)),
    ]

    def prepare(x, g, base):
        turned = x[...].astype(F32).T
        rows[base : base + half, :128] = turned.astype(BF16)
        rows[base : base + half, 128:] = pieces(turned, False)
        pulled = g[...].astype(F32).T
        grads[base : base + half, :] = jnp.concatenate([pulled, pulled], axis=1).astype(BF16)
        wide[:128, base : base + half] = x[...]

    prepare(x_ref, g_ref, 0)
    wide[128:, :] = (lax.broadcasted_iota(jnp.int32, (16, 2 * chip), 0) == 0).astype(F32).astype(BF16)
    for c in z_in:
        c.wait_recv()
    incoming = {}

    def offer(*blocks):
        for i in blocks:
            incoming[i] = go(remote(marks.at[0], marks.at[i], g_s.at[i], g_r.at[i], in_plane(i, -1)))

    offer(1, 2, 3, 4)
    x_in.wait_recv()
    g_in.wait_recv()
    prepare(mate_x, mate_g, half)
    offer(5, 6, 7, 8)

    scale = factor * math.log2(math.e)

    def mark_rows(p):
        return marks[2 * p : 2 * p + 2, 0:2].reshape(256, 128)

    def weigh(p, base):
        plain = mark_rows(p)
        near = jnp.concatenate([plain, pieces(plain.astype(F32), True)], axis=1)
        pull = []
        for i in (2 * p, 2 * p + 1):
            packed = marks[i, 2]
            lane = lax.broadcasted_iota(jnp.int32, packed.shape, 1)
            zero = jnp.zeros_like(packed)
            pull += [jnp.where(lane < 64, packed, zero), jnp.where(lane < 64, zero, packed)]
        pull = jnp.concatenate(pull, axis=0)
        cross = lax.dot_general(rows[base : base + chip, :], near, LAST, preferred_element_type=F32)
        pulled = lax.dot_general(grads[base : base + chip, :], pull, LAST, preferred_element_type=F32)
        weights[p, base : base + chip, :] = (pulled * jnp.exp2(cross * scale)).astype(BF16)

    def backward(p):
        total = jnp.dot(wide[...], weights[p], preferred_element_type=F32).T
        return total[:, :128] - mark_rows(p).astype(F32) * total[:, 128:129]

    reduce1 = {}

    def finish(p):
        total = backward(p)
        for i in (2 * p, 2 * p + 1):
            block = total[(i % 2) * 128 : (i % 2) * 128 + 128]
            if i:
                send1[i] = block.astype(BF16)
            else:
                own[...] = block

    def ship(p):
        for i in (2 * p, 2 * p + 1):
            if i:
                reduce1[i] = go(remote(send1.at[i], recv1.at[i], r1_s.at[i], r1_r.at[i], in_plane(i, 1)))

    def arrived(p):
        for i in (2 * p, 2 * p + 1):
            if i:
                incoming[i].wait_recv()

    ones = (lax.broadcasted_iota(jnp.int32, (256, 128), 1) == 0).astype(F32).astype(BF16)

    def toward(r):
        total = jnp.zeros((PASS, 256), F32)
        for p in range(8):
            total = total + jnp.dot(
                weights[p, r : r + PASS, :], jnp.concatenate([mark_rows(p), ones], axis=1), preferred_element_type=F32
            )
        return total[:, :128] - rows[r : r + PASS, :128].astype(F32) * total[:, 128:129]

    arrived(0)
    arrived(1)
    offer(9, 10, 11)
    weigh(0, 0)
    weigh(1, 0)
    for c in far_in:
        c.wait_recv()
    cross_in = [
        go(remote(far_x, cross_x, c_s.at[4], c_r.at[4], mate)),
        go(remote(far_g, cross_g, c_s.at[5], c_r.at[5], mate)),
    ]
    prepare(far_x, far_g, chip)
    arrived(2)
    arrived(3)
    offer(12, 13, 14, 15)
    weigh(2, 0)
    weigh(3, 0)
    for c in cross_in:
        c.wait_recv()
    prepare(cross_x, cross_g, chip + half)
    for p in range(4):
        weigh(p, chip)
        if p:
            finish(p - 1)
    for p in range(3):
        ship(p)
    arrived(4)
    arrived(5)
    weigh(4, 0)
    finish(3)
    weigh(4, chip)
    weigh(5, 0)
    finish(4)
    weigh(5, chip)
    ship(3)
    ship(4)
    arrived(6)
    arrived(7)
    weigh(6, 0)
    finish(5)
    weigh(6, chip)
    weigh(7, 0)
    finish(6)
    weigh(7, chip)
    ship(5)
    ship(6)
    finish(7)
    ship(7)

    part_in = []
    for n in range(2):
        r = pl.ds(n * PASS, PASS)
        part[r, :] = toward(chip + half + n * PASS)
        part_in.append(go(remote(part.at[r, :], mate_part.at[r, :], t_s.at[n], t_r.at[n], mate)))
    far_back = []

    def send_back(n):
        r = pl.ds(n * PASS, PASS)
        part_in[n].wait_recv()
        send4[r, :] = (mine[r, :] + mate_part[r, :]).astype(BF16)
        far_back.append(go(remote(send4.at[r, :], recv4.at[r, :], t_s.at[2 + n], t_r.at[2 + n], far)))

    mine[:PASS, :] = toward(chip)
    send_back(0)
    mine[PASS:, :] = toward(chip + PASS)
    for r in range(0, half, PASS):
        back[r : r + PASS, :] = toward(half + r)
    t_in = go(remote(back, mate_back, t_s.at[4], t_r.at[4], mate))

    for i in range(1, 16):
        reduce1[i].wait_recv()
    total = own[...]
    for i in range(1, 16):
        total = total + recv1[i].astype(F32)
    send3[...] = total.reshape(2, 64, 128)
    reduce3 = []
    for d in range(3):
        to = pl.ds(pl.multiple_of((level + d + 1) % 4 * 16, 16), 16)
        reduce3.append(go(remote(send3.at[:, to, :], recv3.at[d], r3_s.at[d], r3_r.at[d], on_z(d + 1))))
    send_back(1)

    for r in range(0, half, PASS):
        mine[r : r + PASS, :] = toward(r)

    for c in reduce3:
        c.wait_recv()
    total = send3[:, at, :]
    for d in range(3):
        total = total + recv3[d]
    gl_ref[...] = factor * total.reshape(32, 128)
    t_in.wait_recv()
    for c in far_back:
        c.wait_recv()
    gf_ref[...] = factor * (mine[...] + mate_back[...] + recv4[...].astype(F32)).T
    for c in sent:
        c.wait_send()


def per_device(features, landmarks, cotangent, eigen_basis, inv_eigen):
    width, count = features.shape
    vmem = pl.BlockSpec(memory_space=pltpu.VMEM)
    dma = pltpu.SemaphoreType.DMA
    grad_features, grad_landmarks = pl.pallas_call(
        functools.partial(kernel, 4.0 / width),
        out_shape=(
            jax.ShapeDtypeStruct(features.shape, F32),
            jax.ShapeDtypeStruct(landmarks.shape[::-1], F32),
        ),
        in_specs=[vmem] * 5,
        out_specs=(vmem, vmem),
        scratch_shapes=[
            pltpu.VMEM((16, 3, 64, 128), BF16),
            pltpu.VMEM((128, count), BF16),
            pltpu.VMEM((64, count), BF16),
            pltpu.VMEM((128, count), BF16),
            pltpu.VMEM((64, count), BF16),
            pltpu.VMEM((128, count), BF16),
            pltpu.VMEM((64, count), BF16),
            pltpu.VMEM((4 * count, 256), BF16),
            pltpu.VMEM((4 * count, 128), BF16),
            pltpu.VMEM((144, 4 * count), BF16),
            pltpu.VMEM((8, 4 * count, 256), BF16),
            pltpu.VMEM((16, 128, 128), BF16),
            pltpu.VMEM((16, 128, 128), BF16),
            pltpu.VMEM((128, 128), F32),
            pltpu.VMEM((2, 64, 128), F32),
            pltpu.VMEM((3, 2, 16, 128), F32),
            pltpu.VMEM((count, 128), F32),
            pltpu.VMEM((count, 128), F32),
            pltpu.VMEM((count, 128), BF16),
            pltpu.VMEM((count, 128), BF16),
            pltpu.VMEM((count, 128), F32),
            pltpu.VMEM((count, 128), F32),
            pltpu.VMEM((count, 128), F32),
            dma((3,)), dma((3,)), dma((6,)), dma((6,)), dma((16,)), dma((16,)),
            dma((16,)), dma((16,)), dma((3,)), dma((3,)), dma((5,)), dma((5,)),
        ],
        compiler_params=pltpu.CompilerParams(
            collective_id=0, has_side_effects=True, vmem_limit_bytes=60 * 2**20
        ),
    )(features, landmarks.T, cotangent, eigen_basis.T, inv_eigen.reshape(1, -1))
    return grad_features, grad_landmarks.T


def solution(mesh):
    return jax.shard_map(
        per_device,
        mesh=mesh,
        in_specs=(
            P(None, ("node", "lm")),
            P(None, ("lm", "node")),
            P(None, ("node", "lm")),
            P(None, ("lm", "node")),
            P(),
        ),
        out_specs=(P(None, ("node", "lm")), P(None, ("lm", "node"))),
        check_vma=False,
    )
```
